32 devices in a mesh: dp: 4 (over y, core), expert: 8 (over z, x).
Axes of the slice: x: 2, y: 2, z: 4, core: 2. Of those that a mesh axis runs over, the one named last changes fastest.
Arguments:
- tokens: bfloat16 [4096, 2048], P(('dp', 'expert')), may hold values from -6 to 6
- expert_ids: int32 [4096, 2], P(('dp', 'expert')), may hold values from 0 to 7, all different within a row; in each aligned block of 128 rows (0 to 127, 128 to 255, ...) at most 48 rows name the same one
- upstream: bfloat16 [4096, 2048], P(('dp', 'expert')), may hold values from -6 to 6
- gain: float32 [2048], replicated, may hold values from 0.5 to 1.5
- router: bfloat16 [2048, 8], replicated, may hold values from -0.125 to 0.125
- gate_weight_matrix: bfloat16 [8, 2048, 1024], P('expert', 'dp'), may hold values from -0.125 to 0.125
- up_weight: bfloat16 [8, 2048, 1024], P('expert', 'dp'), may hold values from -0.125 to 0.125
- down_weight: bfloat16 [8, 1024, 2048], P('expert', None, 'dp'), may hold values from -0.1875 to 0.1875
Outputs:
- mixed: bfloat16 [4096, 2048], P(('dp', 'expert'))
- d_tokens: bfloat16 [4096, 2048], P(('dp', 'expert'))
- gate_weight_gradient: bfloat16 [8, 2048, 1024], P('expert', 'dp')
- up_weight_gradient: bfloat16 [8, 2048, 1024], P('expert', 'dp')
- down_weight_gradient: bfloat16 [8, 1024, 2048], P('expert', None, 'dp')
- d_router: float32 [2048, 8], replicated
- d_gain: float32 [2048], replicated
The draws below stay inside these ranges and needn't reach their ends.
Inputs may be any that keep to these rules, and one draw needn't show every extreme that they name: `expert_ids`: the two experts of a token differ. Among the tokens of one device (aligned blocks of 128 rows) no expert is named more than 48 times, and in some block one expert is named exactly 48 times.
All inputs are finite; a program needn't handle non-finite values.
Results may differ from the reference program's by a relative error of at most 0.014.
Values may be sent and summed in bfloat16 or wider, within the bound.
A program may use at most 128 MiB of HBM per device.

```python
import math
from functools import partial
import jax
import jax.numpy as jnp
import numpy as np
from jax import lax

D = 2048
FE = 1024
TOK_DEV = 128
EXPERT_TOTAL = 8
ROUTE_CEILING = 48
TOKENS = 4096
N_DP = 4
N_EXPERT = 8


def steps_of(stream_key, dims, pieces, smallest, top_value):
    factor_of = 1.0
    for dim, parts in pieces:
        heights = jax.random.uniform(jax.random.fold_in(jax.random.fold_in(stream_key, 6), dim), (parts,), jnp.float32, smallest / len(pieces), top_value / len(pieces))
        factor_of = factor_of * jnp.repeat(jnp.exp(heights), dims[dim] // parts).reshape((-1,) + (1,) * (len(dims) - 1 - dim))
    return factor_of


def assign_block(stream_key, own, number, rows, count, top, most, slope):
    sequence = jax.random.permutation(stream_key, count)
    packed, common = load_shares(count, rows * top, most, slope, True), load_shares(count, rows * top, most, slope, False)
    places = jnp.arange(count)

    def named(tallies, rotation):
        used = int((tallies > 0).sum())
        fixed = max(1, used // 4)
        passed = fixed + (places - fixed + rotation * (used - fixed)) % max(1, count - fixed)
        return jnp.zeros((count,), jnp.int32).at[sequence[jnp.where(places < fixed, places, passed)]].set(jnp.asarray(tallies, jnp.int32))

    tallies = jnp.where(number % 4 == 0, named(packed, number // 4), named(common, number - number // 4 - 1))
    mixed = jax.random.permutation(jax.random.fold_in(own, 3), count)
    giver, receiver = mixed[0:count // 2 * 2:2], mixed[1:count // 2 * 2:2]
    slack = jnp.minimum(tallies[giver] - 1, most - tallies[receiver]) // 2
    slack = jnp.where((giver == sequence[0]) | (receiver == sequence[0]) | (tallies[receiver] == 0), 0, jnp.maximum(slack, 0))
    passed = jax.random.randint(jax.random.fold_in(own, 4), (count // 2,), 0, 1 << 20) % (slack + 1)
    tallies = tallies.at[giver].add(-passed).at[receiver].add(passed)
    members = jnp.searchsorted(jnp.cumsum(tallies), jnp.arange(rows * top), side="right").astype(jnp.int32)
    listing = members.reshape(top, rows).T
    listing = listing[jax.random.permutation(jax.random.fold_in(own, 1), rows)]
    rotation = jax.random.randint(jax.random.fold_in(own, 2), (rows, 1), 0, top)
    return jnp.take_along_axis(listing, (jnp.arange(top)[None, :] + rotation) % top, axis=1)


def load_shares(number_of, total, bound, skew, full):
    weights = [(1 << 20) // math.isqrt(rank ** skew) + 1 for rank in range(1, number_of + 1)]
    largest = bound if full else min(bound, max(-(-total // number_of), total * weights[0] // sum(weights)))
    least = 1 if total - largest >= number_of - 1 else 0
    given, rest = [largest] + [least] * (number_of - 1), total - largest - least * (number_of - 1)
    while rest > 0:
        candidates = [i for i in range(1, number_of) if given[i] < largest] or [i for i in range(1, number_of) if given[i] < bound]
        pool, remaining = sum([weights[i] for i in candidates]), rest
        for i in candidates:
            addition = min(bound - given[i], max(1, remaining * weights[i] // pool), rest)
            given[i] = given[i] + addition
            rest = rest - addition
    return np.array(given)


def centred(stream_key, shape, scale, reach, pieces=(), kind=jnp.bfloat16):
    result = scale * jax.random.normal(stream_key, shape, jnp.float32)
    if pieces:
        result = result * steps_of(stream_key, shape, pieces, -0.22, 0.18)
    return jnp.clip(result, -reach, reach).astype(kind)


def setup_inputs(seed: int = 0) -> dict:
    keys = jax.random.split(jax.random.key(seed), 9)
    tokens = centred(keys[0], (TOKENS, D), 1.0, 6.0, ((0, 32),))
    expert_ids_keys = jax.random.split(jax.random.fold_in(keys[1], 1), TOKENS // TOK_DEV)
    expert_ids_turns = jax.random.permutation(jax.random.fold_in(keys[1], 3), TOKENS // TOK_DEV)
    expert_ids = jax.vmap(lambda own, number: assign_block(jax.random.fold_in(keys[1], 2), own, number, TOK_DEV, EXPERT_TOTAL, 2, ROUTE_CEILING, 2))(expert_ids_keys, expert_ids_turns).reshape((TOKENS, 2))
    upstream = centred(keys[2], (TOKENS, D), 1.0, 6.0, ((0, 32),))
    gain = jnp.clip(1.0 + 0.1 * jax.random.normal(keys[3], (D,), jnp.float32), 0.5, 1.5)
    router = centred(keys[4], (D, EXPERT_TOTAL), D ** -0.5, 0.125)
    gate_weight_matrix = centred(keys[5], (EXPERT_TOTAL, D, FE), D ** -0.5, 0.125, ((0, 8), (1, 4)))
    up_weight = centred(keys[6], (EXPERT_TOTAL, D, FE), D ** -0.5, 0.125, ((0, 8), (1, 4)))
    down_weight = centred(keys[7], (EXPERT_TOTAL, FE, D), FE ** -0.5, 0.1875, ((0, 8), (2, 4)))
    return {"tokens": tokens, "expert_ids": expert_ids, "upstream": upstream, "gain": gain, "router": router, "gate_weight_matrix": gate_weight_matrix, "up_weight": up_weight, "down_weight": down_weight}


norm_eps = 1e-06

def slot_layout(expert_ids, experts, capacity):
    flattened = expert_ids.reshape(-1)
    onehot = (flattened[:, None] == jnp.arange(experts, dtype=jnp.int32)[None, :]).astype(jnp.int32)
    ranking = lax.optimization_barrier(jnp.sum(jnp.cumsum(onehot, axis=0) * onehot, axis=1)) - 1
    slot_ids = (flattened * capacity + ranking).astype(jnp.int32)
    sources = jnp.zeros((experts * capacity,), jnp.int32).at[slot_ids].set(jnp.arange(flattened.shape[0], dtype=jnp.int32))
    counts = lax.optimization_barrier(jnp.sum(onehot, axis=0))
    slots_occupied = (jnp.arange(capacity, dtype=jnp.int32)[None, :] < counts[:, None]).reshape(-1)
    return (slot_ids, sources, slots_occupied)

def group_sum(left, right):
    left_groups = left.astype(jnp.float32).reshape(N_DP, -1, left.shape[1])
    right_groups = right.astype(jnp.float32).reshape(N_DP, -1, right.shape[1])
    partial_sums = jnp.einsum('pra,prb->pab', left_groups, right_groups).astype(jnp.bfloat16)
    partial_sums = lax.optimization_barrier(partial_sums)
    return lax.optimization_barrier(jnp.sum(partial_sums.astype(jnp.float32), axis=0)).astype(jnp.bfloat16)

def reference(tokens, expert_ids, upstream, gain, router, gate_weight_matrix, up_weight, down_weight):
    source = tokens.astype(jnp.float32)
    inverse = lax.rsqrt(lax.optimization_barrier(jnp.mean(source * source, axis=-1, keepdims=True)) + norm_eps)
    unit_rows = source * inverse
    normed = (unit_rows * gain).astype(jnp.bfloat16)
    scores = jax.nn.sigmoid(jnp.dot(normed, router, preferred_element_type=jnp.float32))
    picked = expert_ids[:, :, None] == jnp.arange(EXPERT_TOTAL, dtype=jnp.int32)[None, None, :]
    chosen = lax.optimization_barrier(jnp.sum(jnp.where(picked, scores[:, None, :], 0.0), axis=2))
    total = lax.optimization_barrier(jnp.sum(chosen, axis=1, keepdims=True))
    gates = chosen / total
    device_list = N_DP * N_EXPERT
    per_device = expert_ids.reshape(device_list, TOK_DEV, 2)
    layout = jax.vmap(partial(slot_layout, experts=EXPERT_TOTAL, capacity=ROUTE_CEILING))
    slot_ids, sources, slots_occupied = layout(per_device)
    offsets = (jnp.arange(device_list, dtype=jnp.int32) * (2 * TOK_DEV))[:, None]
    expert_allotted = (sources + offsets).astype(jnp.int32)
    expert_allotted = expert_allotted.reshape(device_list, EXPERT_TOTAL, ROUTE_CEILING).transpose(1, 0, 2).reshape(EXPERT_TOTAL, device_list * ROUTE_CEILING)
    row_alive_mask = slots_occupied.reshape(device_list, EXPERT_TOTAL, ROUTE_CEILING).transpose(1, 0, 2).reshape(EXPERT_TOTAL, device_list * ROUTE_CEILING).astype(jnp.float32)
    gate_flat = gates.reshape(-1)
    cotangent = upstream.astype(jnp.float32)

    def single_expert(carry, inputs):
        mixture_running, backward_running, gate_gradient_running = carry
        routes, live_rows, gate_w, up_w, down_w = inputs
        token_rows = routes // 2
        rows = normed[token_rows] * live_rows[:, None].astype(jnp.bfloat16)
        pre_gate = jnp.dot(rows, gate_w, preferred_element_type=jnp.float32)
        pre_up = jnp.dot(rows, up_w, preferred_element_type=jnp.float32)
        sigma = jax.nn.sigmoid(pre_gate)
        active = pre_gate * sigma
        hidden = (active * pre_up).astype(jnp.bfloat16)
        expert_out = jnp.dot(hidden, down_w, preferred_element_type=jnp.float32).astype(jnp.bfloat16)
        weight = gate_flat[routes] * live_rows
        cot_rows = cotangent[token_rows]
        d_out = (weight[:, None] * cot_rows).astype(jnp.bfloat16)
        dgate_rows = lax.optimization_barrier(jnp.sum(cot_rows * expert_out.astype(jnp.float32), axis=1)) * live_rows
        d_hidden = jnp.dot(d_out, down_w.T, preferred_element_type=jnp.float32)
        d_pre_gate = (d_hidden * pre_up * sigma * (1.0 + pre_gate * (1.0 - sigma))).astype(jnp.bfloat16)
        d_pre_up = (d_hidden * active).astype(jnp.bfloat16)
        d_rows = (jnp.dot(d_pre_gate, gate_w.T, preferred_element_type=jnp.float32) + jnp.dot(d_pre_up, up_w.T, preferred_element_type=jnp.float32)).astype(jnp.bfloat16)
        mixture_running = mixture_running.at[token_rows].add(weight[:, None] * expert_out.astype(jnp.float32))
        backward_running = backward_running.at[token_rows].add(d_rows.astype(jnp.float32) * live_rows[:, None])
        gate_gradient_running = gate_gradient_running.at[routes].add(dgate_rows)
        grads = (group_sum(rows, d_pre_gate), group_sum(rows, d_pre_up), group_sum(hidden, d_out))
        return ((mixture_running, backward_running, gate_gradient_running), grads)
    begin_offset = (jnp.zeros((TOKENS, D), jnp.float32), jnp.zeros((TOKENS, D), jnp.float32), jnp.zeros((TOKENS * 2,), jnp.float32))
    (mixture_running, backward_running, gate_gradient_running), (gate_weight_gradient, up_weight_gradient, down_weight_gradient) = lax.scan(single_expert, begin_offset, (expert_allotted, row_alive_mask, gate_weight_matrix, up_weight, down_weight))
    mixed = (source + mixture_running).astype(jnp.bfloat16)
    d_gates = gate_gradient_running.reshape(TOKENS, 2)
    blended = lax.optimization_barrier(jnp.sum(gates * d_gates, axis=1, keepdims=True))
    d_chosen = (d_gates - blended) / total
    d_logit = d_chosen * chosen * (1.0 - chosen)
    d_logits = lax.optimization_barrier(jnp.sum(jnp.where(picked, d_logit[:, :, None], 0.0), axis=1))
    router_float = router.astype(jnp.float32)
    d_normed = backward_running + jnp.dot(d_logits, router_float.T, precision=lax.Precision.HIGHEST)
    d_unit = d_normed * gain
    inner = lax.optimization_barrier(jnp.mean(d_unit * unit_rows, axis=-1, keepdims=True))
    d_tokens = (cotangent + inverse * (d_unit - unit_rows * inner)).astype(jnp.bfloat16)
    d_router = jnp.dot(normed.astype(jnp.float32).T, d_logits, precision=lax.Precision.HIGHEST)
    d_gain = lax.optimization_barrier(jnp.sum(d_normed * unit_rows, axis=0))
    return (mixed, d_tokens, gate_weight_gradient, up_weight_gradient, down_weight_gradient, d_router, d_gain)
```

```python
import jax
import jax.numpy as jnp
from jax import lax
from jax.sharding import PartitionSpec as P

norm_eps = 1e-06


def product(left, right):
    return jnp.dot(left, right, preferred_element_type=jnp.float32)


def transposed_product(left, right):
    return lax.dot_general(
        left, right, (((1,), (1,)), ((), ())), preferred_element_type=jnp.float32
    )


def inner_product(left, right):
    return lax.dot_general(
        left, right, (((0,), (0,)), ((), ())), preferred_element_type=jnp.float32
    )


def slot_pairs_of(expert_ids, experts, capacity):
    flattened = expert_ids.reshape(-1)
    onehot = (flattened[:, None] == jnp.arange(experts, dtype=jnp.int32)[None, :]).astype(jnp.int32)
    ranking = jnp.sum(jnp.cumsum(onehot, axis=0) * onehot, axis=1) - 1
    return (flattened * capacity + ranking).reshape(expert_ids.shape)


def to_sibling(value):
    count = lax.axis_size("dp")
    return lax.ppermute(value, "dp", [(i, i ^ 1) for i in range(count)])


def to_chip(value, step):
    count = lax.axis_size("dp")
    return lax.ppermute(value, "dp", [(i, (i + 2 * step) % count) for i in range(count)])


def sum_over_all(value):
    for axis in ("dp", "expert"):
        count = lax.axis_size(axis)
        hop = 1
        while hop < count:
            value = value + lax.ppermute(value, axis, [(i, i ^ hop) for i in range(count)])
            hop *= 2
    return value


def on_device(
    tokens, expert_ids, upstream, gain, router, gate_weight_matrix, up_weight, down_weight
):
    experts = lax.axis_size("expert")
    dp_count = lax.axis_size("dp")
    chips = dp_count // 2
    me = lax.axis_index("dp")
    tok_rows, width = tokens.shape
    feed = gate_weight_matrix.shape[2]
    part = width // dp_count
    capacity = 3 * tok_rows // experts
    slots = experts * capacity

    shard = (gate_weight_matrix[0], up_weight[0], down_weight[0])
    pieces = []
    owners = []
    for k in range(chips):
        arrived = shard if k == 0 else tuple(to_chip(w, k) for w in shard)
        pieces.append(arrived)
        pieces.append(tuple(to_sibling(w) for w in arrived))
        owner = lax.rem(me - 2 * k + dp_count, dp_count)
        owners.append(owner)
        owners.append(owner + 1 - 2 * lax.rem(owner, 2))

    source = tokens.astype(jnp.float32)
    inverse = lax.rsqrt(jnp.mean(source * source, axis=-1, keepdims=True) + norm_eps)
    unit_rows = source * inverse
    normed = (unit_rows * gain).astype(jnp.bfloat16)
    scores = jax.nn.sigmoid(product(normed, router))
    picked = expert_ids[:, :, None] == jnp.arange(experts, dtype=jnp.int32)[None, None, :]
    chosen = jnp.sum(jnp.where(picked, scores[:, None, :], 0.0), axis=2)
    total = jnp.sum(chosen, axis=1, keepdims=True)
    gates = chosen / total

    slot_pairs = slot_pairs_of(expert_ids, experts, capacity)
    places = jnp.arange(slots, dtype=jnp.int32)
    first = places[:, None] == slot_pairs[None, :, 0]
    second = places[:, None] == slot_pairs[None, :, 1]
    fill = (first | second).astype(jnp.bfloat16)
    slot_gate = jnp.sum(
        jnp.where(first, gates[None, :, 0], jnp.where(second, gates[None, :, 1], 0.0)),
        axis=1,
        keepdims=True,
    )
    send_rows = product(fill, normed).astype(jnp.bfloat16)
    d_send = (slot_gate * product(fill, upstream)).astype(jnp.bfloat16)
    arrived = lax.all_to_all(
        jnp.concatenate(
            [
                send_rows.reshape(experts, capacity, width),
                d_send.reshape(experts, capacity, width),
            ],
            axis=1,
        ),
        "expert",
        split_axis=0,
        concat_axis=0,
        tiled=True,
    )
    expert_in = arrived[:, :capacity].reshape(slots, width)
    d_out = arrived[:, capacity:].reshape(slots, width)
    in_parts = [lax.dynamic_slice_in_dim(expert_in, o * part, part, 1) for o in owners]
    out_parts = [lax.dynamic_slice_in_dim(d_out, o * part, part, 1) for o in owners]

    pre_gate = sum(product(x, w[0]) for x, w in zip(in_parts, pieces))
    pre_up = sum(product(x, w[1]) for x, w in zip(in_parts, pieces))
    sigma = jax.nn.sigmoid(pre_gate)
    active = pre_gate * sigma
    hidden = (active * pre_up).astype(jnp.bfloat16)

    def in_order(parts):
        whole = jnp.zeros((slots, width), jnp.bfloat16)
        for o, value in zip(owners, parts):
            whole = lax.dynamic_update_slice_in_dim(whole, value, o * part, 1)
        return whole

    def send_back(rows):
        return lax.all_to_all(
            rows.reshape(experts, capacity, width),
            "expert",
            split_axis=0,
            concat_axis=0,
            tiled=True,
        ).reshape(slots, width)

    expert_out = in_order([product(hidden, w[2]).astype(jnp.bfloat16) for w in pieces])
    returned = send_back(expert_out)

    d_hidden = sum(transposed_product(x, w[2]) for x, w in zip(out_parts, pieces))
    d_pre_gate = (d_hidden * pre_up * sigma * (1.0 + pre_gate * (1.0 - sigma))).astype(jnp.bfloat16)
    d_pre_up = (d_hidden * active).astype(jnp.bfloat16)

    def shares(index):
        x, d = in_parts[index], out_parts[index]
        return (
            inner_product(x, d_pre_gate).astype(jnp.bfloat16),
            inner_product(x, d_pre_up).astype(jnp.bfloat16),
            inner_product(hidden, d).astype(jnp.bfloat16),
        )

    totals = None
    for k in list(range(1, chips)) + [0]:
        theirs = [to_sibling(v) for v in shares(2 * k + 1)]
        mine = shares(2 * k)
        both = [a.astype(jnp.float32) + b.astype(jnp.float32) for a, b in zip(mine, theirs)]
        if k:
            both = [
                to_chip(v.astype(jnp.bfloat16), chips - k).astype(jnp.float32) for v in both
            ]
        totals = both if totals is None else [a + b for a, b in zip(totals, both)]
    weight_gradients = [v.astype(jnp.bfloat16)[None] for v in totals]

    d_rows = in_order(
        [
            (transposed_product(d_pre_gate, w[0]) + transposed_product(d_pre_up, w[1])).astype(
                jnp.bfloat16
            )
            for w in pieces
        ]
    )
    d_back = send_back(d_rows)

    cotangent = upstream.astype(jnp.float32)
    first_out = inner_product(first.astype(jnp.bfloat16), returned)
    second_out = inner_product(second.astype(jnp.bfloat16), returned)
    mixed = (source + gates[:, :1] * first_out + gates[:, 1:] * second_out).astype(jnp.bfloat16)
    d_gates = jnp.concatenate(
        [
            jnp.sum(cotangent * first_out, axis=1, keepdims=True),
            jnp.sum(cotangent * second_out, axis=1, keepdims=True),
        ],
        axis=1,
    )
    blended = jnp.sum(gates * d_gates, axis=1, keepdims=True)
    d_chosen = (d_gates - blended) / total
    d_logit = d_chosen * chosen * (1.0 - chosen)
    d_logits = jnp.sum(jnp.where(picked, d_logit[:, :, None], 0.0), axis=1)
    part_router = lax.dot_general(
        d_logits,
        normed.astype(jnp.float32),
        (((0,), (0,)), ((), ())),
        precision=lax.Precision.HIGHEST,
    )
    d_router = sum_over_all(part_router).T
    through_router = jnp.dot(
        d_logits, router.astype(jnp.float32).T, precision=lax.Precision.HIGHEST
    )

    d_normed = inner_product(fill, d_back) + through_router
    d_unit = d_normed * gain
    inner = jnp.mean(d_unit * unit_rows, axis=-1, keepdims=True)
    d_tokens = (cotangent + inverse * (d_unit - unit_rows * inner)).astype(jnp.bfloat16)
    part_gain = jnp.sum(d_normed * unit_rows, axis=0)
    d_gain = sum_over_all(part_gain.reshape(-1, 128)).reshape(-1)
    return (mixed, d_tokens, *weight_gradients, d_router, d_gain)


def solution(mesh):
    return jax.shard_map(
        on_device,
        mesh=mesh,
        in_specs=(
            P(("dp", "expert"), None),
            P(("dp", "expert"), None),
            P(("dp", "expert"), None),
            P(),
            P(),
            P("expert", "dp", None),
            P("expert", "dp", None),
            P("expert", None, "dp"),
        ),
        out_specs=(
            P(("dp", "expert"), None),
            P(("dp", "expert"), None),
            P("expert", "dp", None),
            P("expert", "dp", None),
            P("expert", None, "dp"),
            P(),
            P(),
        ),
        check_vma=False,
    )
```

```python
import jax
import jax.numpy as jnp
from jax import lax
from jax.sharding import PartitionSpec as P

norm_eps = 1e-06


def product(left, right):
    return jnp.dot(left, right, preferred_element_type=jnp.float32)


def transposed_product(left, right):
    return lax.dot_general(
        left, right, (((1,), (1,)), ((), ())), preferred_element_type=jnp.float32
    )


def inner_product(left, right):
    return lax.dot_general(
        left, right, (((0,), (0,)), ((), ())), preferred_element_type=jnp.float32
    )


def slot_pairs_of(expert_ids, experts, capacity):
    flattened = expert_ids.reshape(-1)
    onehot = (flattened[:, None] == jnp.arange(experts, dtype=jnp.int32)[None, :]).astype(jnp.int32)
    ranking = jnp.sum(jnp.cumsum(onehot, axis=0) * onehot, axis=1) - 1
    return (flattened * capacity + ranking).reshape(expert_ids.shape)


def to_sibling(value):
    count = lax.axis_size("dp")
    return lax.ppermute(value, "dp", [(i, i ^ 1) for i in range(count)])


def to_chip(value, step):
    count = lax.axis_size("dp")
    return lax.ppermute(value, "dp", [(i, i ^ (2 * step)) for i in range(count)])


def sum_over_all(value):
    for axis in ("dp", "expert"):
        count = lax.axis_size(axis)

        def at(mask):
            return lax.ppermute(value, axis, [(i, i ^ mask) for i in range(count)])

        hop = 1
        while hop < count:
            if 4 * hop <= count:
                value = (value + at(hop)) + (at(2 * hop) + at(3 * hop))
                hop *= 4
            else:
                value = value + at(hop)
                hop *= 2
    return value


def on_device(
    tokens, expert_ids, upstream, gain, router, gate_weight_matrix, up_weight, down_weight
):
    experts = lax.axis_size("expert")
    dp_count = lax.axis_size("dp")
    chips = dp_count // 2
    me = lax.axis_index("dp")
    tok_rows, width = tokens.shape
    feed = gate_weight_matrix.shape[2]
    part = width // dp_count
    capacity = 3 * tok_rows // experts
    slots = experts * capacity

    shard = (gate_weight_matrix[0], up_weight[0], down_weight[0])
    pieces = []
    for k in range(chips):
        arrived = shard if k == 0 else tuple(to_chip(w, k) for w in shard)
        pieces.append(arrived)
        pieces.append(tuple(to_sibling(w) for w in arrived))

    def reordered(value):
        return jnp.concatenate(
            [lax.dynamic_slice_in_dim(value, (me ^ p) * part, part, 1) for p in range(dp_count)],
            axis=1,
        )

    def split(value):
        return [value[:, p * part : (p + 1) * part] for p in range(dp_count)]

    source = tokens.astype(jnp.float32)
    inverse = lax.rsqrt(jnp.mean(source * source, axis=-1, keepdims=True) + norm_eps)
    unit_rows = source * inverse
    normed = (unit_rows * gain).astype(jnp.bfloat16)
    scores = jax.nn.sigmoid(product(normed, router))
    picked = expert_ids[:, :, None] == jnp.arange(experts, dtype=jnp.int32)[None, None, :]
    chosen = jnp.sum(jnp.where(picked, scores[:, None, :], 0.0), axis=2)
    total = jnp.sum(chosen, axis=1, keepdims=True)
    gates = chosen / total

    slot_pairs = slot_pairs_of(expert_ids, experts, capacity)
    places = jnp.arange(slots, dtype=jnp.int32)
    first = places[:, None] == slot_pairs[None, :, 0]
    second = places[:, None] == slot_pairs[None, :, 1]
    fill = (first | second).astype(jnp.bfloat16)
    slot_gate = jnp.sum(
        jnp.where(first, gates[None, :, 0], jnp.where(second, gates[None, :, 1], 0.0)),
        axis=1,
        keepdims=True,
    )
    def exchange(rows):
        return lax.all_to_all(
            rows.reshape(experts, capacity, width),
            "expert",
            split_axis=0,
            concat_axis=0,
            tiled=True,
        ).reshape(slots, width)

    expert_in = exchange(product(fill, reordered(normed)).astype(jnp.bfloat16))
    d_out = exchange((slot_gate * product(fill, reordered(upstream))).astype(jnp.bfloat16))
    in_parts = split(expert_in)

    pre_gate = sum(product(x, w[0]) for x, w in zip(in_parts, pieces))
    pre_up = sum(product(x, w[1]) for x, w in zip(in_parts, pieces))
    sigma = jax.nn.sigmoid(pre_gate)
    active = pre_gate * sigma
    hidden = (active * pre_up).astype(jnp.bfloat16)

    expert_out = jnp.concatenate(
        [product(hidden, w[2]).astype(jnp.bfloat16) for w in pieces], axis=1
    )
    expert_out, d_out, hidden = lax.optimization_barrier((expert_out, d_out, hidden))
    returned = exchange(expert_out)
    out_parts = split(d_out)

    d_hidden = sum(transposed_product(x, w[2]) for x, w in zip(out_parts, pieces))
    d_pre_gate = (d_hidden * pre_up * sigma * (1.0 + pre_gate * (1.0 - sigma))).astype(jnp.bfloat16)
    d_pre_up = (d_hidden * active).astype(jnp.bfloat16)

    def shares(index):
        x, d = in_parts[index], out_parts[index]
        return (
            inner_product(x, d_pre_gate).astype(jnp.bfloat16),
            inner_product(x, d_pre_up).astype(jnp.bfloat16),
            inner_product(hidden, d).astype(jnp.bfloat16),
        )

    def pair_sum(k):
        theirs = [to_sibling(v) for v in shares(2 * k + 1)]
        return [
            a.astype(jnp.float32) + b.astype(jnp.float32) for a, b in zip(shares(2 * k), theirs)
        ]

    away = [[v.astype(jnp.bfloat16) for v in pair_sum(k)] for k in range(1, chips)]
    totals = pair_sum(0)
    away, d_pre_gate, d_pre_up = lax.optimization_barrier((away, d_pre_gate, d_pre_up))
    d_rows = jnp.concatenate(
        [
            (transposed_product(d_pre_gate, w[0]) + transposed_product(d_pre_up, w[1])).astype(
                jnp.bfloat16
            )
            for w in pieces
        ],
        axis=1,
    )
    d_back = exchange(d_rows)
    for k in range(1, chips):
        landed = [to_chip(v, k).astype(jnp.float32) for v in away[k - 1]]
        totals = [a + b for a, b in zip(totals, landed)]
    weight_gradients = [v.astype(jnp.bfloat16)[None] for v in totals]

    cotangent = upstream.astype(jnp.float32)
    first_out = reordered(inner_product(first.astype(jnp.bfloat16), returned))
    second_out = reordered(inner_product(second.astype(jnp.bfloat16), returned))
    mixed = (source + gates[:, :1] * first_out + gates[:, 1:] * second_out).astype(jnp.bfloat16)
    d_gates = jnp.concatenate(
        [
            jnp.sum(cotangent * first_out, axis=1, keepdims=True),
            jnp.sum(cotangent * second_out, axis=1, keepdims=True),
        ],
        axis=1,
    )
    blended = jnp.sum(gates * d_gates, axis=1, keepdims=True)
    d_chosen = (d_gates - blended) / total
    d_logit = d_chosen * chosen * (1.0 - chosen)
    d_logits = jnp.sum(jnp.where(picked, d_logit[:, :, None], 0.0), axis=1)
    part_router = lax.dot_general(
        d_logits,
        normed.astype(jnp.float32),
        (((0,), (0,)), ((), ())),
        precision=lax.Precision.HIGHEST,
    )
    through_router = jnp.dot(
        d_logits, router.astype(jnp.float32).T, precision=lax.Precision.HIGHEST
    )

    d_normed = reordered(inner_product(fill, d_back)) + through_router
    d_unit = d_normed * gain
    inner = jnp.mean(d_unit * unit_rows, axis=-1, keepdims=True)
    d_tokens = (cotangent + inverse * (d_unit - unit_rows * inner)).astype(jnp.bfloat16)
    part_gain = jnp.sum(d_normed * unit_rows, axis=0)
    summed = sum_over_all(jnp.concatenate([part_router, part_gain[None]], axis=0))
    d_router = summed[:experts].T
    d_gain = summed[experts]
    return (mixed, d_tokens, *weight_gradients, d_router, d_gain)


def solution(mesh):
    return jax.shard_map(
        on_device,
        mesh=mesh,
        in_specs=(
            P(("dp", "expert"), None),
            P(("dp", "expert"), None),
            P(("dp", "expert"), None),
            P(),
            P(),
            P("expert", "dp", None),
            P("expert", "dp", None),
            P("expert", None, "dp"),
        ),
        out_specs=(
            P(("dp", "expert"), None),
            P(("dp", "expert"), None),
            P("expert", "dp", None),
            P("expert", "dp", None),
            P("expert", None, "dp"),
            P(),
            P(),
        ),
        check_vma=False,
    )
```

```python
import functools

import jax
import jax.numpy as jnp
from jax import lax
from jax.experimental import pallas as pl
from jax.experimental.pallas import tpu as pltpu
from jax.sharding import PartitionSpec as P

norm_eps = 1e-06
MESH = pl.DeviceIdType.MESH


def product(left, right):
    return jnp.dot(left, right, preferred_element_type=jnp.float32)


def transposed_product(left, right):
    return lax.dot_general(
        left, right, (((1,), (1,)), ((), ())), preferred_element_type=jnp.float32
    )


def inner_product(left, right):
    return lax.dot_general(
        left, right, (((0,), (0,)), ((), ())), preferred_element_type=jnp.float32
    )


def slot_pairs_of(expert_ids, experts, capacity):
    flattened = expert_ids.reshape(-1)
    onehot = (flattened[:, None] == jnp.arange(experts, dtype=jnp.int32)[None, :]).astype(jnp.int32)
    ranking = jnp.sum(jnp.cumsum(onehot, axis=0) * onehot, axis=1) - 1
    return (flattened * capacity + ranking).reshape(expert_ids.shape)


def to_sibling(value):
    count = lax.axis_size("dp")
    return lax.ppermute(value, "dp", [(i, i ^ 1) for i in range(count)])


def to_chip(value, step):
    count = lax.axis_size("dp")
    return lax.ppermute(value, "dp", [(i, i ^ (2 * step)) for i in range(count)])


def exchange_sum_kernel(n, m, v_ref, o_ref, near, far, mine, send_sem, recv_sem):
    d, e = lax.axis_index("dp"), lax.axis_index("expert")
    cols = v_ref.shape[1] // n
    barrier = pltpu.get_barrier_semaphore()
    dp_peers = [lax.rem(d + p, n) for p in range(1, n)]
    ex_peers = [lax.rem(e + p, m) for p in range(1, m)]
    for peer in dp_peers:
        pl.semaphore_signal(barrier, inc=1, device_id=(peer, e), device_id_type=MESH)
    for peer in ex_peers:
        pl.semaphore_signal(barrier, inc=1, device_id=(d, peer), device_id_type=MESH)
    pl.semaphore_wait(barrier, n + m - 2)

    def chunk(ref, index):
        return ref.at[:, pl.ds(pl.multiple_of(index * cols, cols), cols)]

    def send(src, dst, sem, device):
        copy = pltpu.make_async_remote_copy(
            src_ref=src,
            dst_ref=dst,
            send_sem=send_sem.at[sem],
            recv_sem=recv_sem.at[sem],
            device_id=device,
            device_id_type=MESH,
        )
        copy.start()
        return copy

    copies = [
        send(chunk(v_ref, peer), near.at[i], i, (peer, e)) for i, peer in enumerate(dp_peers)
    ]
    value = v_ref[:, pl.ds(pl.multiple_of(d * cols, cols), cols)]
    for i, copy in enumerate(copies):
        copy.wait()
        value = value + near[i]
    mine[...] = value
    far[e] = value
    copies = [
        send(mine, far.at[e], n - 1 + i, (d, peer)) for i, peer in enumerate(ex_peers)
    ]
    for copy in copies:
        copy.wait()
    value = far[0]
    for i in range(1, m):
        value = value + far[i]
    mine[...] = value
    o_ref[:, pl.ds(pl.multiple_of(d * cols, cols), cols)] = value
    copies = [
        send(mine, chunk(o_ref, d), n + m - 2 + i, (peer, e)) for i, peer in enumerate(dp_peers)
    ]
    for copy in copies:
        copy.wait()


def sum_over_all(value):
    n, m = lax.axis_size("dp"), lax.axis_size("expert")
    rows, width = value.shape
    part = width // n
    flights = 2 * (n - 1) + m - 1
    return pl.pallas_call(
        functools.partial(exchange_sum_kernel, n, m),
        out_shape=jax.ShapeDtypeStruct((rows, width), jnp.float32),
        in_specs=[pl.BlockSpec(memory_space=pltpu.VMEM)],
        out_specs=pl.BlockSpec(memory_space=pltpu.VMEM),
        scratch_shapes=[
            pltpu.VMEM((n - 1, rows, part), jnp.float32),
            pltpu.VMEM((m, rows, part), jnp.float32),
            pltpu.VMEM((rows, part), jnp.float32),
            pltpu.SemaphoreType.DMA((flights,)),
            pltpu.SemaphoreType.DMA((flights,)),
        ],
        compiler_params=pltpu.CompilerParams(collective_id=0, has_side_effects=True),
        cost_estimate=pl.CostEstimate(
            flops=rows * width * (n + m), bytes_accessed=8 * rows * width * n, transcendentals=0
        ),
    )(value)


def on_device(
    tokens, expert_ids, upstream, gain, router, gate_weight_matrix, up_weight, down_weight
):
    experts = lax.axis_size("expert")
    dp_count = lax.axis_size("dp")
    chips = dp_count // 2
    me = lax.axis_index("dp")
    tok_rows, width = tokens.shape
    feed = gate_weight_matrix.shape[2]
    part = width // dp_count
    capacity = 3 * tok_rows // experts
    slots = experts * capacity

    shard = (gate_weight_matrix[0], up_weight[0], down_weight[0])
    pieces = []
    for k in range(chips):
        arrived = shard if k == 0 else tuple(to_chip(w, k) for w in shard)
        pieces.append(arrived)
        pieces.append(tuple(to_sibling(w) for w in arrived))

    def reordered(value):
        return jnp.concatenate(
            [lax.dynamic_slice_in_dim(value, (me ^ p) * part, part, 1) for p in range(dp_count)],
            axis=1,
        )

    def split(value):
        return [value[:, p * part : (p + 1) * part] for p in range(dp_count)]

    source = tokens.astype(jnp.float32)
    inverse = lax.rsqrt(jnp.mean(source * source, axis=-1, keepdims=True) + norm_eps)
    unit_rows = source * inverse
    normed = (unit_rows * gain).astype(jnp.bfloat16)
    scores = jax.nn.sigmoid(product(normed, router))
    picked = expert_ids[:, :, None] == jnp.arange(experts, dtype=jnp.int32)[None, None, :]
    chosen = jnp.sum(jnp.where(picked, scores[:, None, :], 0.0), axis=2)
    total = jnp.sum(chosen, axis=1, keepdims=True)
    gates = chosen / total

    slot_pairs = slot_pairs_of(expert_ids, experts, capacity)
    places = jnp.arange(slots, dtype=jnp.int32)
    first = places[:, None] == slot_pairs[None, :, 0]
    second = places[:, None] == slot_pairs[None, :, 1]
    fill = (first | second).astype(jnp.bfloat16)
    slot_gate = jnp.sum(
        jnp.where(first, gates[None, :, 0], jnp.where(second, gates[None, :, 1], 0.0)),
        axis=1,
        keepdims=True,
    )
    def exchange(rows):
        return lax.all_to_all(
            rows.reshape(experts, capacity, width),
            "expert",
            split_axis=0,
            concat_axis=0,
            tiled=True,
        ).reshape(slots, width)

    expert_in = exchange(product(fill, reordered(normed)).astype(jnp.bfloat16))
    d_out = exchange((slot_gate * product(fill, reordered(upstream))).astype(jnp.bfloat16))
    d_out, pieces[2:] = lax.optimization_barrier((d_out, pieces[2:]))
    in_parts = split(expert_in)

    pre_gate = sum(product(x, w[0]) for x, w in zip(in_parts, pieces))
    pre_up = sum(product(x, w[1]) for x, w in zip(in_parts, pieces))
    sigma = jax.nn.sigmoid(pre_gate)
    active = pre_gate * sigma
    hidden = (active * pre_up).astype(jnp.bfloat16)

    expert_out = jnp.concatenate(
        [product(hidden, w[2]).astype(jnp.bfloat16) for w in pieces], axis=1
    )
    expert_out, d_out, hidden = lax.optimization_barrier((expert_out, d_out, hidden))
    returned = exchange(expert_out)
    out_parts = split(d_out)

    d_hidden = sum(transposed_product(x, w[2]) for x, w in zip(out_parts, pieces))
    d_pre_gate = (d_hidden * pre_up * sigma * (1.0 + pre_gate * (1.0 - sigma))).astype(jnp.bfloat16)
    d_pre_up = (d_hidden * active).astype(jnp.bfloat16)

    def shares(index):
        x, d = in_parts[index], out_parts[index]
        return (
            inner_product(x, d_pre_gate).astype(jnp.bfloat16),
            inner_product(x, d_pre_up).astype(jnp.bfloat16),
            inner_product(hidden, d).astype(jnp.bfloat16),
        )

    def pair_sum(k):
        theirs = [to_sibling(v) for v in shares(2 * k + 1)]
        return [
            a.astype(jnp.float32) + b.astype(jnp.float32) for a, b in zip(shares(2 * k), theirs)
        ]

    away = [[v.astype(jnp.bfloat16) for v in pair_sum(k)] for k in range(1, chips)]
    totals = pair_sum(0)
    landed = [[to_chip(v, k) for v in away[k - 1]] for k in range(1, chips)]
    away, returned, d_pre_gate, d_pre_up = lax.optimization_barrier(
        (away, returned, d_pre_gate, d_pre_up)
    )
    d_rows = jnp.concatenate(
        [
            (transposed_product(d_pre_gate, w[0]) + transposed_product(d_pre_up, w[1])).astype(
                jnp.bfloat16
            )
            for w in pieces
        ],
        axis=1,
    )
    if chips > 1:
        d_rows, landed[0][0] = lax.optimization_barrier((d_rows, landed[0][0]))
        returned, landed[0][2] = lax.optimization_barrier((returned, landed[0][2]))
    d_back = exchange(d_rows)
    if chips > 1:
        d_back, landed[0][1] = lax.optimization_barrier((d_back, landed[0][1]))
    for shares_landed in landed:
        totals = [a + b.astype(jnp.float32) for a, b in zip(totals, shares_landed)]
    weight_gradients = [v.astype(jnp.bfloat16)[None] for v in totals]

    cotangent = upstream.astype(jnp.float32)
    first_out = reordered(inner_product(first.astype(jnp.bfloat16), returned))
    second_out = reordered(inner_product(second.astype(jnp.bfloat16), returned))
    mixed = (source + gates[:, :1] * first_out + gates[:, 1:] * second_out).astype(jnp.bfloat16)
    d_gates = jnp.concatenate(
        [
            jnp.sum(cotangent * first_out, axis=1, keepdims=True),
            jnp.sum(cotangent * second_out, axis=1, keepdims=True),
        ],
        axis=1,
    )
    blended = jnp.sum(gates * d_gates, axis=1, keepdims=True)
    d_chosen = (d_gates - blended) / total
    d_logit = d_chosen * chosen * (1.0 - chosen)
    d_logits = jnp.sum(jnp.where(picked, d_logit[:, :, None], 0.0), axis=1)
    part_router = lax.dot_general(
        d_logits,
        normed.astype(jnp.float32),
        (((0,), (0,)), ((), ())),
        precision=lax.Precision.HIGHEST,
    )
    through_router = jnp.dot(
        d_logits, router.astype(jnp.float32).T, precision=lax.Precision.HIGHEST
    )

    d_normed = reordered(inner_product(fill, d_back)) + through_router
    d_unit = d_normed * gain
    inner = jnp.mean(d_unit * unit_rows, axis=-1, keepdims=True)
    d_tokens = (cotangent + inverse * (d_unit - unit_rows * inner)).astype(jnp.bfloat16)
    part_gain = jnp.sum((d_normed * unit_rows).reshape(-1, 8, width), axis=0)
    summed = sum_over_all(jnp.concatenate([part_router, part_gain], axis=0))
    d_router = summed[:experts].T
    d_gain = jnp.sum(summed[experts:], axis=0)
    return (mixed, d_tokens, *weight_gradients, d_router, d_gain)


def solution(mesh):
    return jax.shard_map(
        on_device,
        mesh=mesh,
        in_specs=(
            P(("dp", "expert"), None),
            P(("dp", "expert"), None),
            P(("dp", "expert"), None),
            P(),
            P(),
            P("expert", "dp", None),
            P("expert", "dp", None),
            P("expert", None, "dp"),
        ),
        out_specs=(
            P(("dp", "expert"), None),
            P(("dp", "expert"), None),
            P("expert", "dp", None),
            P("expert", "dp", None),
            P("expert", None, "dp"),
            P(),
            P(),
        ),
        check_vma=False,
    )
```

```python
import functools

import jax
import jax.numpy as jnp
from jax import lax
from jax.experimental import pallas as pl
from jax.experimental.pallas import tpu as pltpu
from jax.sharding import PartitionSpec as P

norm_eps = 1e-06
MESH = pl.DeviceIdType.MESH


def product(left, right):
    return jnp.dot(left, right, preferred_element_type=jnp.float32)


def transposed_product(left, right):
    return lax.dot_general(
        left, right, (((1,), (1,)), ((), ())), preferred_element_type=jnp.float32
    )


def inner_product(left, right):
    return lax.dot_general(
        left, right, (((0,), (0,)), ((), ())), preferred_element_type=jnp.float32
    )


def slot_pairs_of(expert_ids, experts, capacity):
    flattened = expert_ids.reshape(-1)
    onehot = (flattened[:, None] == jnp.arange(experts, dtype=jnp.int32)[None, :]).astype(jnp.int32)
    ranking = jnp.sum(jnp.cumsum(onehot, axis=0) * onehot, axis=1) - 1
    return (flattened * capacity + ranking).reshape(expert_ids.shape)


def to_sibling(value):
    count = lax.axis_size("dp")
    return lax.ppermute(value, "dp", [(i, i ^ 1) for i in range(count)])


def to_chip(value, step):
    count = lax.axis_size("dp")
    return lax.ppermute(value, "dp", [(i, i ^ (2 * step)) for i in range(count)])


def exchange_sum_kernel(n, m, v_ref, o_ref, near, far, mine, send_sem, recv_sem):
    d, e = lax.axis_index("dp"), lax.axis_index("expert")
    cols = v_ref.shape[1] // n
    barrier = pltpu.get_barrier_semaphore()
    dp_peers = [lax.rem(d + p, n) for p in range(1, n)]
    ex_peers = [lax.rem(e + p, m) for p in range(1, m)]
    for peer in dp_peers:
        pl.semaphore_signal(barrier, inc=1, device_id=(peer, e), device_id_type=MESH)
    for peer in ex_peers:
        pl.semaphore_signal(barrier, inc=1, device_id=(d, peer), device_id_type=MESH)
    pl.semaphore_wait(barrier, n + m - 2)

    def chunk(ref, index):
        return ref.at[:, pl.ds(pl.multiple_of(index * cols, cols), cols)]

    def send(src, dst, sem, device):
        copy = pltpu.make_async_remote_copy(
            src_ref=src,
            dst_ref=dst,
            send_sem=send_sem.at[sem],
            recv_sem=recv_sem.at[sem],
            device_id=device,
            device_id_type=MESH,
        )
        copy.start()
        return copy

    copies = [
        send(chunk(v_ref, peer), near.at[i], i, (peer, e)) for i, peer in enumerate(dp_peers)
    ]
    value = v_ref[:, pl.ds(pl.multiple_of(d * cols, cols), cols)]
    for i, copy in enumerate(copies):
        copy.wait()
        value = value + near[i]
    mine[...] = value
    far[e] = value
    copies = [
        send(mine, far.at[e], n - 1 + i, (d, peer)) for i, peer in enumerate(ex_peers)
    ]
    for copy in copies:
        copy.wait()
    value = far[0]
    for i in range(1, m):
        value = value + far[i]
    mine[...] = value
    o_ref[:, pl.ds(pl.multiple_of(d * cols, cols), cols)] = value
    copies = [
        send(mine, chunk(o_ref, d), n + m - 2 + i, (peer, e)) for i, peer in enumerate(dp_peers)
    ]
    for copy in copies:
        copy.wait()


def sum_over_all(value):
    n, m = lax.axis_size("dp"), lax.axis_size("expert")
    rows, width = value.shape
    part = width // n
    flights = 2 * (n - 1) + m - 1
    return pl.pallas_call(
        functools.partial(exchange_sum_kernel, n, m),
        out_shape=jax.ShapeDtypeStruct((rows, width), jnp.float32),
        in_specs=[pl.BlockSpec(memory_space=pltpu.VMEM)],
        out_specs=pl.BlockSpec(memory_space=pltpu.VMEM),
        scratch_shapes=[
            pltpu.VMEM((n - 1, rows, part), jnp.float32),
            pltpu.VMEM((m, rows, part), jnp.float32),
            pltpu.VMEM((rows, part), jnp.float32),
            pltpu.SemaphoreType.DMA((flights,)),
            pltpu.SemaphoreType.DMA((flights,)),
        ],
        compiler_params=pltpu.CompilerParams(collective_id=0, has_side_effects=True),
        cost_estimate=pl.CostEstimate(
            flops=rows * width * (n + m), bytes_accessed=8 * rows * width * n, transcendentals=0
        ),
    )(value)


def on_device(
    tokens, expert_ids, upstream, gain, router, gate_weight_matrix, up_weight, down_weight
):
    experts = lax.axis_size("expert")
    dp_count = lax.axis_size("dp")
    chips = dp_count // 2
    me = lax.axis_index("dp")
    tok_rows, width = tokens.shape
    feed = gate_weight_matrix.shape[2]
    part = width // dp_count
    capacity = 3 * tok_rows // experts
    slots = experts * capacity

    shard = (gate_weight_matrix[0], up_weight[0], down_weight[0])
    pieces = []
    for k in range(chips):
        arrived = shard if k == 0 else tuple(to_chip(w, k) for w in shard)
        pieces.append(arrived)
        pieces.append(tuple(to_sibling(w) for w in arrived))

    def reordered(value):
        return jnp.concatenate(
            [lax.dynamic_slice_in_dim(value, (me ^ p) * part, part, 1) for p in range(dp_count)],
            axis=1,
        )

    def split(value):
        return [value[:, p * part : (p + 1) * part] for p in range(dp_count)]

    source = tokens.astype(jnp.float32)
    inverse = lax.rsqrt(jnp.mean(source * source, axis=-1, keepdims=True) + norm_eps)
    unit_rows = source * inverse
    normed = (unit_rows * gain).astype(jnp.bfloat16)
    scores = jax.nn.sigmoid(product(normed, router))
    picked = expert_ids[:, :, None] == jnp.arange(experts, dtype=jnp.int32)[None, None, :]
    chosen = jnp.sum(jnp.where(picked, scores[:, None, :], 0.0), axis=2)
    total = jnp.sum(chosen, axis=1, keepdims=True)
    gates = chosen / total

    slot_pairs = slot_pairs_of(expert_ids, experts, capacity)
    places = jnp.arange(slots, dtype=jnp.int32)
    first = places[:, None] == slot_pairs[None, :, 0]
    second = places[:, None] == slot_pairs[None, :, 1]
    fill = (first | second).astype(jnp.bfloat16)
    slot_gate = jnp.sum(
        jnp.where(first, gates[None, :, 0], jnp.where(second, gates[None, :, 1], 0.0)),
        axis=1,
        keepdims=True,
    )
    def exchange(rows):
        return lax.all_to_all(
            rows.reshape(experts, capacity, width),
            "expert",
            split_axis=0,
            concat_axis=0,
            tiled=True,
        ).reshape(slots, width)

    arrived = lax.all_to_all(
        jnp.concatenate(
            [
                rows.reshape(experts, capacity, width)
                for rows in (
                    product(fill, reordered(normed)).astype(jnp.bfloat16),
                    (slot_gate * product(fill, reordered(upstream))).astype(jnp.bfloat16),
                )
            ],
            axis=1,
        ),
        "expert",
        split_axis=0,
        concat_axis=0,
        tiled=True,
    )
    expert_in = arrived[:, :capacity].reshape(slots, width)
    d_out = arrived[:, capacity:].reshape(slots, width)
    in_parts = split(expert_in)

    pre_gate = sum(product(x, w[0]) for x, w in zip(in_parts, pieces))
    pre_up = sum(product(x, w[1]) for x, w in zip(in_parts, pieces))
    sigma = jax.nn.sigmoid(pre_gate)
    active = pre_gate * sigma
    hidden = (active * pre_up).astype(jnp.bfloat16)

    expert_out = jnp.concatenate(
        [product(hidden, w[2]).astype(jnp.bfloat16) for w in pieces], axis=1
    )
    expert_out, d_out, hidden = lax.optimization_barrier((expert_out, d_out, hidden))
    returned = exchange(expert_out)
    out_parts = split(d_out)

    d_hidden = sum(transposed_product(x, w[2]) for x, w in zip(out_parts, pieces))
    d_pre_gate = (d_hidden * pre_up * sigma * (1.0 + pre_gate * (1.0 - sigma))).astype(jnp.bfloat16)
    d_pre_up = (d_hidden * active).astype(jnp.bfloat16)

    def pair_sum(lefts, rights, k, waited=()):
        theirs = to_sibling(inner_product(lefts[2 * k + 1], rights[2 * k + 1]).astype(jnp.bfloat16))
        theirs, waited = lax.optimization_barrier((theirs, waited))
        mine = inner_product(lefts[2 * k], rights[2 * k]).astype(jnp.bfloat16)
        return mine.astype(jnp.float32) + theirs.astype(jnp.float32)

    def from_chips(lefts, rights, waited=()):
        return [
            to_chip(pair_sum(lefts, rights, k, waited).astype(jnp.bfloat16), k)
            for k in range(1, chips)
        ]

    hiddens, d_gates_in, d_ups_in = ([v] * dp_count for v in (hidden, d_pre_gate, d_pre_up))
    landed_down = from_chips(hiddens, out_parts)
    landed_gate = from_chips(in_parts, d_gates_in, landed_down)
    landed_up = from_chips(in_parts, d_ups_in, landed_down)

    def d_rows_of(w, d_gate, d_up):
        return (transposed_product(d_gate, w[0]) + transposed_product(d_up, w[1])).astype(
            jnp.bfloat16
        )

    d_rows = [d_rows_of(pieces[0], d_pre_gate, d_pre_up)]
    returned, late_gate, late_up = lax.optimization_barrier((returned, d_pre_gate, d_pre_up))
    d_rows += [d_rows_of(w, late_gate, late_up) for w in pieces[1:]]
    d_rows, landed_gate = lax.optimization_barrier((d_rows, landed_gate))
    d_back = exchange(jnp.concatenate(d_rows, axis=1))
    d_back, landed_up = lax.optimization_barrier((d_back, landed_up))
    totals = [
        sum((v.astype(jnp.float32) for v in landed), pair_sum(lefts, rights, 0))
        for landed, lefts, rights in (
            (landed_gate, in_parts, d_gates_in),
            (landed_up, in_parts, d_ups_in),
            (landed_down, hiddens, out_parts),
        )
    ]
    weight_gradients = [v.astype(jnp.bfloat16)[None] for v in totals]

    cotangent = upstream.astype(jnp.float32)
    first_out = reordered(inner_product(first.astype(jnp.bfloat16), returned))
    second_out = reordered(inner_product(second.astype(jnp.bfloat16), returned))
    mixed = (source + gates[:, :1] * first_out + gates[:, 1:] * second_out).astype(jnp.bfloat16)
    d_gates = jnp.concatenate(
        [
            jnp.sum(cotangent * first_out, axis=1, keepdims=True),
            jnp.sum(cotangent * second_out, axis=1, keepdims=True),
        ],
        axis=1,
    )
    blended = jnp.sum(gates * d_gates, axis=1, keepdims=True)
    d_chosen = (d_gates - blended) / total
    d_logit = d_chosen * chosen * (1.0 - chosen)
    d_logits = jnp.sum(jnp.where(picked, d_logit[:, :, None], 0.0), axis=1)
    part_router = lax.dot_general(
        d_logits,
        normed.astype(jnp.float32),
        (((0,), (0,)), ((), ())),
        precision=lax.Precision.HIGHEST,
    )
    through_router = jnp.dot(
        d_logits, router.astype(jnp.float32).T, precision=lax.Precision.HIGHEST
    )

    d_normed = reordered(inner_product(fill, d_back)) + through_router
    d_unit = d_normed * gain
    inner = jnp.mean(d_unit * unit_rows, axis=-1, keepdims=True)
    d_tokens = (cotangent + inverse * (d_unit - unit_rows * inner)).astype(jnp.bfloat16)
    part_gain = jnp.sum((d_normed * unit_rows).reshape(-1, 8, width), axis=0)
    summed = sum_over_all(jnp.concatenate([part_router, part_gain], axis=0))
    d_router = summed[:experts].T
    d_gain = jnp.sum(summed[experts:], axis=0)
    return (mixed, d_tokens, *weight_gradients, d_router, d_gain)


def solution(mesh):
    return jax.shard_map(
        on_device,
        mesh=mesh,
        in_specs=(
            P(("dp", "expert"), None),
            P(("dp", "expert"), None),
            P(("dp", "expert"), None),
            P(),
            P(),
            P("expert", "dp", None),
            P("expert", "dp", None),
            P("expert", None, "dp"),
        ),
        out_specs=(
            P(("dp", "expert"), None),
            P(("dp", "expert"), None),
            P("expert", "dp", None),
            P("expert", "dp", None),
            P("expert", None, "dp"),
            P(),
            P(),
        ),
        check_vma=False,
    )
```

```python
import functools

import jax
import jax.numpy as jnp
from jax import lax
from jax.experimental import pallas as pl
from jax.experimental.pallas import tpu as pltpu
from jax.sharding import PartitionSpec as P

norm_eps = 1e-06
MESH = pl.DeviceIdType.MESH


def product(left, right):
    return jnp.dot(left, right, preferred_element_type=jnp.float32)


def transposed_product(left, right):
    return lax.dot_general(
        left, right, (((1,), (1,)), ((), ())), preferred_element_type=jnp.float32
    )


def inner_product(left, right):
    return lax.dot_general(
        left, right, (((0,), (0,)), ((), ())), preferred_element_type=jnp.float32
    )


def slot_pairs_of(expert_ids, experts, capacity):
    flattened = expert_ids.reshape(-1)
    onehot = (flattened[:, None] == jnp.arange(experts, dtype=jnp.int32)[None, :]).astype(jnp.int32)
    ranking = jnp.sum(jnp.cumsum(onehot, axis=0) * onehot, axis=1) - 1
    return (flattened * capacity + ranking).reshape(expert_ids.shape)


def to_sibling(value):
    count = lax.axis_size("dp")
    return lax.ppermute(value, "dp", [(i, i ^ 1) for i in range(count)])


def to_chip(value, step):
    count = lax.axis_size("dp")
    return lax.ppermute(value, "dp", [(i, i ^ (2 * step)) for i in range(count)])


def exchange_sum_kernel(n, m, v_ref, o_ref, near, far, mine, send_sem, recv_sem):
    d, e = lax.axis_index("dp"), lax.axis_index("expert")
    cols = v_ref.shape[1] // n
    barrier = pltpu.get_barrier_semaphore()
    dp_peers = [lax.rem(d + p, n) for p in range(1, n)]
    ex_peers = [lax.rem(e + p, m) for p in range(1, m)]
    for peer in dp_peers:
        pl.semaphore_signal(barrier, inc=1, device_id=(peer, e), device_id_type=MESH)
    for peer in ex_peers:
        pl.semaphore_signal(barrier, inc=1, device_id=(d, peer), device_id_type=MESH)
    pl.semaphore_wait(barrier, n + m - 2)

    def chunk(ref, index):
        return ref.at[:, pl.ds(pl.multiple_of(index * cols, cols), cols)]

    def send(src, dst, sem, device):
        copy = pltpu.make_async_remote_copy(
            src_ref=src,
            dst_ref=dst,
            send_sem=send_sem.at[sem],
            recv_sem=recv_sem.at[sem],
            device_id=device,
            device_id_type=MESH,
        )
        copy.start()
        return copy

    copies = [
        send(chunk(v_ref, peer), near.at[i], i, (peer, e)) for i, peer in enumerate(dp_peers)
    ]
    value = v_ref[:, pl.ds(pl.multiple_of(d * cols, cols), cols)]
    for i, copy in enumerate(copies):
        copy.wait()
        value = value + near[i]
    mine[...] = value
    far[e] = value
    copies = [
        send(mine, far.at[e], n - 1 + i, (d, peer)) for i, peer in enumerate(ex_peers)
    ]
    for copy in copies:
        copy.wait()
    value = far[0]
    for i in range(1, m):
        value = value + far[i]
    mine[...] = value
    o_ref[:, pl.ds(pl.multiple_of(d * cols, cols), cols)] = value
    copies = [
        send(mine, chunk(o_ref, d), n + m - 2 + i, (peer, e)) for i, peer in enumerate(dp_peers)
    ]
    for copy in copies:
        copy.wait()


def sum_over_all(value):
    n, m = lax.axis_size("dp"), lax.axis_size("expert")
    rows, width = value.shape
    part = width // n
    flights = 2 * (n - 1) + m - 1
    return pl.pallas_call(
        functools.partial(exchange_sum_kernel, n, m),
        out_shape=jax.ShapeDtypeStruct((rows, width), jnp.float32),
        in_specs=[pl.BlockSpec(memory_space=pltpu.VMEM)],
        out_specs=pl.BlockSpec(memory_space=pltpu.VMEM),
        scratch_shapes=[
            pltpu.VMEM((n - 1, rows, part), jnp.float32),
            pltpu.VMEM((m, rows, part), jnp.float32),
            pltpu.VMEM((rows, part), jnp.float32),
            pltpu.SemaphoreType.DMA((flights,)),
            pltpu.SemaphoreType.DMA((flights,)),
        ],
        compiler_params=pltpu.CompilerParams(collective_id=0, has_side_effects=True),
        cost_estimate=pl.CostEstimate(
            flops=rows * width * (n + m), bytes_accessed=8 * rows * width * n, transcendentals=0
        ),
    )(value)


def on_device(
    tokens, expert_ids, upstream, gain, router, gate_weight_matrix, up_weight, down_weight
):
    experts = lax.axis_size("expert")
    dp_count = lax.axis_size("dp")
    chips = dp_count // 2
    me = lax.axis_index("dp")
    tok_rows, width = tokens.shape
    feed = gate_weight_matrix.shape[2]
    part = width // dp_count
    capacity = 3 * tok_rows // experts
    slots = experts * capacity

    shard = (gate_weight_matrix[0], up_weight[0], down_weight[0])
    pieces = []
    for k in range(chips):
        arrived = shard if k == 0 else tuple(to_chip(w, k) for w in shard)
        pieces.append(arrived)
        pieces.append(tuple(to_sibling(w) for w in arrived))

    def reordered(value):
        return jnp.concatenate(
            [lax.dynamic_slice_in_dim(value, (me ^ p) * part, part, 1) for p in range(dp_count)],
            axis=1,
        )

    def split(value):
        return [value[:, p * part : (p + 1) * part] for p in range(dp_count)]

    source = tokens.astype(jnp.float32)
    inverse = lax.rsqrt(jnp.mean(source * source, axis=-1, keepdims=True) + norm_eps)
    unit_rows = source * inverse
    normed = (unit_rows * gain).astype(jnp.bfloat16)
    scores = jax.nn.sigmoid(product(normed, router))
    picked = expert_ids[:, :, None] == jnp.arange(experts, dtype=jnp.int32)[None, None, :]
    chosen = jnp.sum(jnp.where(picked, scores[:, None, :], 0.0), axis=2)
    total = jnp.sum(chosen, axis=1, keepdims=True)
    gates = chosen / total

    slot_pairs = slot_pairs_of(expert_ids, experts, capacity)
    places = jnp.arange(slots, dtype=jnp.int32)
    first = places[:, None] == slot_pairs[None, :, 0]
    second = places[:, None] == slot_pairs[None, :, 1]
    fill = (first | second).astype(jnp.bfloat16)
    slot_gate = jnp.sum(
        jnp.where(first, gates[None, :, 0], jnp.where(second, gates[None, :, 1], 0.0)),
        axis=1,
        keepdims=True,
    )
    def exchange(rows):
        return lax.all_to_all(
            rows.reshape(experts, capacity, width),
            "expert",
            split_axis=0,
            concat_axis=0,
            tiled=True,
        ).reshape(slots, width)

    arrived = lax.all_to_all(
        jnp.concatenate(
            [
                rows.reshape(experts, capacity, width)
                for rows in (
                    product(fill, reordered(normed)).astype(jnp.bfloat16),
                    (slot_gate * product(fill, reordered(upstream))).astype(jnp.bfloat16),
                )
            ],
            axis=1,
        ),
        "expert",
        split_axis=0,
        concat_axis=0,
        tiled=True,
    )
    expert_in = arrived[:, :capacity].reshape(slots, width)
    d_out = arrived[:, capacity:].reshape(slots, width)
    in_parts = split(expert_in)

    pre_gate = sum(product(x, w[0]) for x, w in zip(in_parts, pieces))
    pre_up = sum(product(x, w[1]) for x, w in zip(in_parts, pieces))
    sigma = jax.nn.sigmoid(pre_gate)
    active = pre_gate * sigma
    hidden = (active * pre_up).astype(jnp.bfloat16)

    expert_out = jnp.concatenate(
        [product(hidden, w[2]).astype(jnp.bfloat16) for w in pieces], axis=1
    )
    expert_out, d_out, hidden = lax.optimization_barrier((expert_out, d_out, hidden))
    returned = exchange(expert_out)
    out_parts = split(d_out)

    d_hidden = sum(transposed_product(x, w[2]) for x, w in zip(out_parts, pieces))
    d_pre_gate = (d_hidden * pre_up * sigma * (1.0 + pre_gate * (1.0 - sigma))).astype(jnp.bfloat16)
    d_pre_up = (d_hidden * active).astype(jnp.bfloat16)

    def pair_sum(lefts, rights, k):
        theirs = to_sibling(inner_product(lefts[2 * k + 1], rights[2 * k + 1]).astype(jnp.bfloat16))
        mine = inner_product(lefts[2 * k], rights[2 * k]).astype(jnp.bfloat16)
        return mine.astype(jnp.float32) + theirs.astype(jnp.float32)

    def from_chips(lefts, rights):
        return [
            to_chip(pair_sum(lefts, rights, k).astype(jnp.bfloat16), k) for k in range(1, chips)
        ]

    hiddens, d_gates_in, d_ups_in = ([v] * dp_count for v in (hidden, d_pre_gate, d_pre_up))
    landed_down = from_chips(hiddens, out_parts)
    landed_gate = from_chips(in_parts, d_gates_in)
    landed_up = from_chips(in_parts, d_ups_in)

    def d_rows_of(w, d_gate, d_up):
        return (transposed_product(d_gate, w[0]) + transposed_product(d_up, w[1])).astype(
            jnp.bfloat16
        )

    d_rows = [d_rows_of(pieces[0], d_pre_gate, d_pre_up)]
    returned, late_gate, late_up = lax.optimization_barrier((returned, d_pre_gate, d_pre_up))
    d_rows += [d_rows_of(w, late_gate, late_up) for w in pieces[1:]]
    d_rows, landed_down = lax.optimization_barrier((d_rows, landed_down))
    returned, landed_gate = lax.optimization_barrier((returned, landed_gate))
    d_back = exchange(jnp.concatenate(d_rows, axis=1))
    d_back, landed_up = lax.optimization_barrier((d_back, landed_up))
    totals = [
        sum((v.astype(jnp.float32) for v in landed), pair_sum(lefts, rights, 0))
        for landed, lefts, rights in (
            (landed_gate, in_parts, d_gates_in),
            (landed_up, in_parts, d_ups_in),
            (landed_down, hiddens, out_parts),
        )
    ]
    weight_gradients = [v.astype(jnp.bfloat16)[None] for v in totals]

    cotangent = upstream.astype(jnp.float32)
    first_out = reordered(inner_product(first.astype(jnp.bfloat16), returned))
    second_out = reordered(inner_product(second.astype(jnp.bfloat16), returned))
    mixed = (source + gates[:, :1] * first_out + gates[:, 1:] * second_out).astype(jnp.bfloat16)
    d_gates = jnp.concatenate(
        [
            jnp.sum(cotangent * first_out, axis=1, keepdims=True),
            jnp.sum(cotangent * second_out, axis=1, keepdims=True),
        ],
        axis=1,
    )
    blended = jnp.sum(gates * d_gates, axis=1, keepdims=True)
    d_chosen = (d_gates - blended) / total
    d_logit = d_chosen * chosen * (1.0 - chosen)
    d_logits = jnp.sum(jnp.where(picked, d_logit[:, :, None], 0.0), axis=1)
    part_router = lax.dot_general(
        d_logits,
        normed.astype(jnp.float32),
        (((0,), (0,)), ((), ())),
        precision=lax.Precision.HIGHEST,
    )
    through_router = jnp.dot(
        d_logits, router.astype(jnp.float32).T, precision=lax.Precision.HIGHEST
    )

    d_normed = reordered(inner_product(fill, d_back)) + through_router
    d_unit = d_normed * gain
    inner = jnp.mean(d_unit * unit_rows, axis=-1, keepdims=True)
    d_tokens = (cotangent + inverse * (d_unit - unit_rows * inner)).astype(jnp.bfloat16)
    part_gain = jnp.sum((d_normed * unit_rows).reshape(-1, 8, width), axis=0)
    summed = sum_over_all(jnp.concatenate([part_router, part_gain], axis=0))
    d_router = summed[:experts].T
    d_gain = jnp.sum(summed[experts:], axis=0)
    return (mixed, d_tokens, *weight_gradients, d_router, d_gain)


def solution(mesh):
    return jax.shard_map(
        on_device,
        mesh=mesh,
        in_specs=(
            P(("dp", "expert"), None),
            P(("dp", "expert"), None),
            P(("dp", "expert"), None),
            P(),
            P(),
            P("expert", "dp", None),
            P("expert", "dp", None),
            P("expert", None, "dp"),
        ),
        out_specs=(
            P(("dp", "expert"), None),
            P(("dp", "expert"), None),
            P("expert", "dp", None),
            P("expert", "dp", None),
            P("expert", None, "dp"),
            P(),
            P(),
        ),
        check_vma=False,
    )
```
